32 devices in a mesh: dp: 8 (over y, x, core), fsdp: 4 (over z).
Axes of the slice: x: 2, y: 2, z: 4, core: 2. Of those that a mesh axis runs over, the one named last changes fastest.
Arguments:
- page_embed: bfloat16 [20480, 2048], P(('dp', 'fsdp')), may hold values from -6 to 6
- page_slot: int32 [20480], P(('dp', 'fsdp')), may hold values from 0 to 5119, as said below
- doc_ids: int32 [32, 640], P(('dp', 'fsdp')), may hold values from 0 to 9, never falling along the last dimension, each value on 1 to 128 neighbouring positions
- qkv_weight: bfloat16 [3, 2048, 1024], P(None, 'fsdp'), may hold values from -0.125 to 0.125
- out_weight: bfloat16 [1024, 2048], P(None, 'fsdp'), may hold values from -0.1875 to 0.1875
- fig_slot: int32 [512], P(('dp', 'fsdp')), may hold values from 0 to 639
- cap_slot: int32 [512], P(('dp', 'fsdp')), may hold values from 0 to 639
- logit_scale: float32 [1], replicated, may hold values from 10 to 30
- loss_cotangent: float32 [512], P(('dp', 'fsdp')), may hold values from 8 to 64
Outputs:
- page_grad: bfloat16 [20480, 2048], P(('dp', 'fsdp'))
- pair_loss: float32 [512], P(('dp', 'fsdp'))
The draws below stay inside these ranges and needn't reach their ends.
Inputs may be any that keep to these rules, and one draw needn't show every extreme that they name: page_slot // 640 is the dp index of the owner and page_slot % 640 the slot there; within each group every slot is named by exactly one page; one device sends at most 100 pages to one owner, and every device sends exactly 100 to some owners. `doc_ids`: along a device's slots the document number never falls; each of the 10 documents has 1 to 128 slots, one exactly 128. `fig_slot`: a slot of the pair's own device. `cap_slot`: a slot of the pair's own device.
All inputs are finite; a program needn't handle non-finite values.
Results may differ from the reference program's by a relative error of at most 0.017.
Values may be sent and summed in bfloat16 or wider, within the bound.
A program may use at most 192 MiB of HBM per device.

```python
import math
import jax
import jax.numpy as jnp
import numpy as np
from jax import lax

D = 2048
HD = 64
DOC_MAX = 128
PAGES_PER_DEVICE = 640
PAIRS_DEV = 16
HDIM = 1024
DOCS_DEV = 10
PAGES = 20480
PAIRS = 512
N_DP = 8
N_FSDP = 4
DEVICES = 32


def draw_page_slot(key, part):
    dp_count = N_DP
    fsdp_count = N_FSDP
    page_count = PAGES_PER_DEVICE
    unit_count = page_count // (4 * dp_count)
    half_count = dp_count // 2

    def one_group(group_key):
        key_extra, key_shift, key_slots, key_order = jax.random.split(group_key, 4)
        extra_order = jax.random.permutation(key_extra, dp_count)
        extra = jnp.where(extra_order < half_count, 2 * unit_count, 0)
        shift = jax.random.randint(key_shift, (), 0, dp_count)
        source = jnp.arange(dp_count)[:, None]
        owner_col = jnp.arange(dp_count)[None, :]
        counts = 3 * unit_count + extra[(owner_col - source + shift) % dp_count]
        offsets = jnp.cumsum(counts, axis=0) - counts
        starts = jnp.cumsum(counts, axis=1) - counts
        slot_perm = jax.vmap(lambda sub_key: jax.random.permutation(sub_key, page_count))(jax.random.split(key_slots, dp_count))
        page_index = jnp.arange(page_count)
        owner_idx = jnp.sum((starts[:, None, :] <= page_index[None, :, None]).astype(jnp.int32), axis=2) - 1
        start_at = jnp.take_along_axis(starts, owner_idx, axis=1)
        offset_at = jnp.take_along_axis(offsets, owner_idx, axis=1)
        position = offset_at + page_index[None, :] - start_at
        chosen = slot_perm[owner_idx, position]
        global_slot = owner_idx * page_count + chosen
        page_order = jax.vmap(lambda sub_key: jax.random.permutation(sub_key, page_count))(jax.random.split(key_order, dp_count))
        return jnp.take_along_axis(global_slot, page_order, axis=1)
    groups = jax.vmap(one_group)(jax.random.split(jax.random.fold_in(key, 11), fsdp_count))
    return jnp.transpose(groups, (1, 0, 2)).reshape(-1).astype(jnp.int32)


def touch_ends(result, key, smallest, top_value):
    longest = result.shape.index(max(result.shape))
    spots = []
    for shift in (0, 1):
        where = [jax.random.randint(jax.random.fold_in(key, axis), (), 0, length) for axis, length in enumerate(result.shape)]
        where[longest] = (where[longest] + shift) % result.shape[longest]
        spots.append(tuple(where))
    return result.at[spots[0]].set(smallest).at[spots[1]].set(top_value)


def levels(own_key, extent, pieces, least, largest):
    loudness = 1.0
    for dim, shards_of in pieces:
        draws = jax.random.uniform(jax.random.fold_in(jax.random.fold_in(own_key, 6), dim), (shards_of,), jnp.float32, least / len(pieces), largest / len(pieces))
        loudness = loudness * jnp.repeat(jnp.exp(draws), extent[dim] // shards_of).reshape((-1,) + (1,) * (len(extent) - 1 - dim))
    return loudness


def length_profile(amount, total, reach, lean):
    loads = [(1 << 20) // math.isqrt(rank ** lean) + 1 for rank in range(2, amount + 1)]
    rest, holding = total - reach - (amount - 1), [1] * (amount - 1)
    while rest > 0:
        free = [i for i in range(amount - 1) if holding[i] < reach]
        whole, left = sum([loads[i] for i in free]), rest
        for i in free:
            more = min(reach - holding[i], max(1, left * loads[i] // whole), rest)
            holding[i] = holding[i] + more
            rest = rest - more
    return np.array([reach] + holding)


def uneven(own_key, amount, total, reach, slope):
    if amount == 2:
        one = jax.random.randint(own_key, (), max(1, total - reach), min(reach, total - 1) + 1)
        return jnp.stack([one, total - one])
    sizes = jnp.asarray(length_profile(amount, total, reach, slope), jnp.int32)
    couples = (amount - 1) // 2
    source_of, sink = sizes[1:1 + 2 * couples:2], sizes[2:2 + 2 * couples:2]
    room = jnp.minimum(source_of - 1, reach - sink)
    moved = jax.random.randint(jax.random.fold_in(own_key, 1), (couples,), 0, 1 << 20) % (room + 1)
    sizes = sizes.at[1:1 + 2 * couples:2].set(source_of - moved).at[2:2 + 2 * couples:2].set(sink + moved)
    return sizes[jax.random.permutation(jax.random.fold_in(own_key, 2), amount)]


def bell_draw(own_key, shape, width, limit, cuts=(), kind=jnp.bfloat16):
    array = width * jax.random.normal(own_key, shape, jnp.float32)
    if cuts:
        array = array * levels(own_key, shape, cuts, -0.22, 0.18)
    return jnp.clip(array, -limit, limit).astype(kind)


def setup_inputs(seed: int = 0) -> dict:
    streams_of = jax.random.split(jax.random.key(seed), 10)
    page_embed = bell_draw(streams_of[0], (PAGES, D), 1.0, 6.0, ((0, 32),))
    page_slot = draw_page_slot(jax.random.fold_in(streams_of[9], 71), 0)
    doc_ids = jax.vmap(lambda own: jnp.searchsorted(jnp.cumsum(uneven(own, DOCS_DEV, PAGES_PER_DEVICE, DOC_MAX, 1)), jnp.arange(PAGES_PER_DEVICE), side="right"))(jax.random.split(streams_of[2], DEVICES)).reshape((DEVICES, PAGES_PER_DEVICE)).astype(jnp.int32)
    qkv_weight = bell_draw(streams_of[3], (3, D, HDIM), D ** -0.5, 0.125, ((1, 4),))
    out_weight = bell_draw(streams_of[4], (HDIM, D), HDIM ** -0.5, 0.1875, ((1, 4),))
    fig_slot = touch_ends(jax.random.randint(streams_of[5], (PAIRS,), 0, PAGES_PER_DEVICE), jax.random.fold_in(streams_of[5], 1), 0, PAGES_PER_DEVICE - 1).astype(jnp.int32)
    cap_slot = touch_ends(jax.random.randint(streams_of[6], (PAIRS,), 0, PAGES_PER_DEVICE), jax.random.fold_in(streams_of[6], 1), 0, PAGES_PER_DEVICE - 1).astype(jnp.int32)
    logit_scale = jnp.clip(jax.random.uniform(streams_of[7], (1,), jnp.float32, 10.0, 30.0), 10.0, 30.0)
    loss_cotangent = jnp.clip(jnp.exp(math.log(64.0) - 2.0794415 * jax.random.uniform(streams_of[8], (PAIRS,), jnp.float32) ** levels(streams_of[8], (PAIRS,), ((0, 32),), -0.2, 0.2)), 8.0, 64.0)
    return {"page_embed": page_embed, "page_slot": page_slot, "doc_ids": doc_ids, "qkv_weight": qkv_weight, "out_weight": out_weight, "fig_slot": fig_slot, "cap_slot": cap_slot, "logit_scale": logit_scale, "loss_cotangent": loss_cotangent}


EPSILON = 1e-06

def log_total(values, axis):
    return jnp.log(lax.optimization_barrier(jnp.sum(jnp.exp(values), axis=axis)))

def attend(slot_row_block, qkv_mat, out_mat, doc_row):
    row_count = slot_row_block.shape[0]
    query_h = jnp.dot(slot_row_block, qkv_mat[0], preferred_element_type=jnp.float32).astype(jnp.bfloat16).reshape(row_count, -1, HD)
    key_h = jnp.dot(slot_row_block, qkv_mat[1], preferred_element_type=jnp.float32).astype(jnp.bfloat16).reshape(row_count, -1, HD)
    value_h = jnp.dot(slot_row_block, qkv_mat[2], preferred_element_type=jnp.float32).astype(jnp.bfloat16).reshape(row_count, -1, HD)
    scores = jnp.einsum('qhd,khd->hqk', query_h.astype(jnp.float32), key_h.astype(jnp.float32)) * (1.0 / math.sqrt(HD))
    same_doc = doc_row[:, None] == doc_row[None, :]
    scores = jnp.where(same_doc[None], scores, -1e+30)
    weights = jnp.exp(scores)
    attn_prob = (weights / lax.optimization_barrier(jnp.sum(weights, axis=2, keepdims=True))).astype(jnp.bfloat16)
    mixed = jnp.einsum('hqk,khd->qhd', attn_prob.astype(jnp.float32), value_h.astype(jnp.float32))
    mixed = mixed.astype(jnp.bfloat16).reshape(row_count, -1)
    return jnp.dot(mixed, out_mat, preferred_element_type=jnp.float32)

def reference(page_embed, page_slot, doc_ids, qkv_weight, out_weight, fig_slot, cap_slot, logit_scale, loss_cotangent):
    feature_width = page_embed.shape[1]
    group_pages = page_embed.reshape(N_DP, N_FSDP, PAGES_PER_DEVICE, feature_width).transpose(1, 0, 2, 3).reshape(N_FSDP, N_DP * PAGES_PER_DEVICE, feature_width)
    group_dest = page_slot.reshape(N_DP, N_FSDP, PAGES_PER_DEVICE).transpose(1, 0, 2).reshape(N_FSDP, N_DP * PAGES_PER_DEVICE)
    group_docs = doc_ids.reshape(N_DP, N_FSDP, PAGES_PER_DEVICE).transpose(1, 0, 2)
    group_fig = fig_slot.reshape(N_DP, N_FSDP, PAIRS_DEV).transpose(1, 0, 2)
    group_cap = cap_slot.reshape(N_DP, N_FSDP, PAIRS_DEV).transpose(1, 0, 2)
    group_weight = loss_cotangent.reshape(N_DP, N_FSDP, PAIRS_DEV).transpose(1, 0, 2)
    logit_mult = logit_scale[0]
    pair_total = N_DP * PAIRS_DEV

    def one_group(group_arguments):
        pages_gradient, destination_gradient, document_gradient, figure_gradient, caption_gradient, weight_gradient = group_arguments
        slot_row_block = jnp.zeros_like(pages_gradient).at[destination_gradient].set(pages_gradient).reshape(N_DP, PAGES_PER_DEVICE, feature_width)

        def forward_pass(entry_args):
            owner_rows, doc_row = entry_args
            return owner_rows.astype(jnp.float32) + attend(owner_rows, qkv_weight, out_weight, doc_row)
        slot_output = lax.map(forward_pass, (slot_row_block, document_gradient))
        fig_vec = jnp.take_along_axis(slot_output, figure_gradient[:, :, None], axis=1).reshape(pair_total, feature_width)
        cap_vec = jnp.take_along_axis(slot_output, caption_gradient[:, :, None], axis=1).reshape(pair_total, feature_width)
        fig_inv = lax.rsqrt(lax.optimization_barrier(jnp.sum(fig_vec * fig_vec, axis=1, keepdims=True)) + EPSILON)
        cap_inv = lax.rsqrt(lax.optimization_barrier(jnp.sum(cap_vec * cap_vec, axis=1, keepdims=True)) + EPSILON)
        fig_unit = fig_vec * fig_inv
        cap_unit = cap_vec * cap_inv
        fig_emb = fig_unit.astype(jnp.bfloat16)
        cap_emb = cap_unit.astype(jnp.bfloat16)
        logits = logit_mult * jnp.dot(fig_emb, cap_emb.T, preferred_element_type=jnp.float32)
        row_lse = log_total(logits, 1)
        col_lse = log_total(logits, 0)
        diag_logit = jnp.diagonal(logits)
        pair_loss = 0.5 * (row_lse - diag_logit) + 0.5 * (col_lse - diag_logit)
        eye_mat = jnp.eye(pair_total, dtype=jnp.float32)
        pair_weight = weight_gradient.reshape(-1)
        prob_rows = jnp.exp(logits - row_lse[:, None])
        prob_cols = jnp.exp(logits - col_lse[None, :])
        coef = 0.5 * pair_weight[:, None] * (prob_rows - eye_mat) + 0.5 * (prob_cols - eye_mat) * pair_weight[None, :]
        fig_grad = logit_mult * jnp.dot(coef, cap_emb.astype(jnp.float32), precision=lax.Precision.HIGHEST)
        cap_grad = logit_mult * jnp.dot(coef.T, fig_emb.astype(jnp.float32), precision=lax.Precision.HIGHEST)
        figure_direction = fig_inv * (fig_grad - fig_unit * lax.optimization_barrier(jnp.sum(fig_unit * fig_grad, axis=1, keepdims=True)))
        caption_direction = cap_inv * (cap_grad - cap_unit * lax.optimization_barrier(jnp.sum(cap_unit * cap_grad, axis=1, keepdims=True)))
        figure_direction = figure_direction.reshape(N_DP, PAIRS_DEV, feature_width)
        caption_direction = caption_direction.reshape(N_DP, PAIRS_DEV, feature_width)

        def backward_pass(entry_args):
            owner_rows, doc_row, fig_idx, cap_idx, fig_part, cap_part = entry_args
            slot_ct = jnp.zeros((PAGES_PER_DEVICE, feature_width), jnp.float32).at[fig_idx].add(fig_part).at[cap_idx].add(cap_part)

            def branch(inputs):
                return attend(inputs, qkv_weight, out_weight, doc_row)
            attn_out, pullback = jax.vjp(branch, owner_rows)
            branch_ct = pullback(slot_ct)[0]
            return (slot_ct + branch_ct.astype(jnp.float32)).astype(jnp.bfloat16)
        slot_gradient = lax.map(backward_pass, (slot_row_block, document_gradient, figure_gradient, caption_gradient, figure_direction, caption_direction)).reshape(N_DP * PAGES_PER_DEVICE, feature_width)
        return (slot_gradient[destination_gradient], pair_loss.reshape(N_DP, PAIRS_DEV))
    grads, losses = lax.map(one_group, (group_pages, group_dest, group_docs, group_fig, group_cap, group_weight))
    page_grad = grads.reshape(N_FSDP, N_DP, PAGES_PER_DEVICE, feature_width).transpose(1, 0, 2, 3).reshape(-1, feature_width)
    pair_loss = losses.transpose(1, 0, 2).reshape(-1)
    return (page_grad, pair_loss)
```

```python
import math

import jax
import jax.numpy as jnp
from jax import lax
from jax.sharding import PartitionSpec as P

HD = 64
EPSILON = 1e-06
FIXED = 2.0**20
BF = jnp.bfloat16
F32 = jnp.float32


def mm(a, b):
    return jnp.dot(a, b, preferred_element_type=F32)


def mmt(a, b):
    return lax.dot_general(a, b, (((1,), (1,)), ((), ())), preferred_element_type=F32)


def tmm(a, b):
    return lax.dot_general(a, b, (((0,), (0,)), ((), ())), preferred_element_type=F32)


def split3(x):
    hi = x.astype(BF)
    rest = x - hi.astype(F32)
    mid = rest.astype(BF)
    low = (rest - mid.astype(F32)).astype(BF)
    return jnp.concatenate([hi, mid, low], axis=0)


def exact_mm(x, emb):
    count = x.shape[0]
    parts = mm(split3(x), emb)
    return parts[:count] + parts[count : 2 * count] + parts[2 * count :]


def expand(x, head_mask):
    return (x[None] * head_mask.astype(x.dtype)).reshape(-1, x.shape[1])


def collapse(x, head_mask, rows):
    return jnp.sum(x.reshape(-1, rows, x.shape[1]) * head_mask, axis=0)


def body(
    page_embed,
    page_slot,
    doc_ids,
    qkv_weight,
    out_weight,
    fig_slot,
    cap_slot,
    logit_scale,
    loss_cotangent,
):
    dp_count = lax.axis_size("dp")
    me = lax.axis_index("dp")
    half = me % 2
    row_count, width = page_embed.shape
    capacity = -(-(5 * row_count) // (4 * dp_count))
    capacity = -(-capacity // 8) * 8
    total = dp_count * capacity
    pair_count = fig_slot.shape[0]
    hdim = qkv_weight.shape[2]
    half_width = hdim // 2
    pair_swap = [(i, i ^ 1) for i in range(dp_count)]

    def gather_half(index):
        piece = lax.dynamic_slice_in_dim(qkv_weight[index], half * half_width, half_width, 1)
        return lax.all_gather(piece, "fsdp", axis=0, tiled=True)

    key_m, query_m, value_m = gather_half(1), gather_half(0), gather_half(2)
    key_o, query_o, value_o = [lax.ppermute(w, "dp", pair_swap) for w in (key_m, query_m, value_m)]
    out_rows = hdim // dp_count
    out_piece = lax.dynamic_slice_in_dim(out_weight, me * out_rows, out_rows, 0)
    out_piece = lax.all_gather(out_piece, "fsdp", axis=1, tiled=True)
    out_full = lax.all_gather(out_piece, "dp", axis=0, tiled=True)

    owner_idx = page_slot // row_count
    slot_idx = page_slot % row_count
    onehot = (owner_idx[:, None] == jnp.arange(dp_count)[None, :]).astype(jnp.int32)
    rank_idx = jnp.sum((jnp.cumsum(onehot, axis=0) - onehot) * onehot, axis=1)
    place_idx = owner_idx * capacity + rank_idx
    place = jnp.arange(total)[:, None] == place_idx[None, :]
    send_ids = jnp.sum(jnp.where(place, slot_idx[None, :] + 1, 0), axis=1) - 1
    fixed_ct = (loss_cotangent * FIXED).astype(jnp.int32)
    send_ints = jnp.concatenate(
        [
            send_ids.reshape(dp_count, capacity),
            jnp.broadcast_to(fixed_ct[None, :], (dp_count, pair_count)),
        ],
        axis=1,
    )
    recv_ints = lax.all_to_all(send_ints, "dp", split_axis=0, concat_axis=0, tiled=True)
    send_rows = mm(place.astype(BF), page_embed).astype(BF)
    rows = lax.all_to_all(send_rows, "dp", split_axis=0, concat_axis=0, tiled=True)

    ids = recv_ints[:, :capacity].reshape(-1)
    group_ct = recv_ints[:, capacity:].reshape(-1).astype(F32) * (1.0 / FIXED)
    doc_row = doc_ids[0]
    slot_range = jnp.arange(row_count)
    row_docs = (
        jnp.sum(jnp.where(ids[:, None] == slot_range[None, :], doc_row[None, :] + 1, 0), axis=1) - 1
    )
    slots = jnp.concatenate([fig_slot, cap_slot])
    slot_docs = jnp.sum(jnp.where(slots[:, None] == slot_range[None, :], doc_row[None, :], 0), axis=1)
    picked = (slots[:, None] == ids[None, :]).astype(BF)
    same_doc = slot_docs[:, None] == row_docs[None, :]
    pick_count = slots.shape[0]

    picked_rows = mm(picked, rows).astype(BF)
    scale = 1.0 / math.sqrt(HD)
    heads = half_width // HD
    head_mask = (
        jnp.arange(half_width)[None, None, :] // HD == jnp.arange(heads)[:, None, None]
    ).astype(F32)

    state = []
    mixes = []
    for w_q, w_k, w_v in ((query_m, key_m, value_m), (query_o, key_o, value_o)):
        key = mm(rows, w_k).astype(BF)
        query = expand(mm(picked_rows, w_q).astype(BF), head_mask)
        value = mm(rows, w_v).astype(BF)
        scores = mmt(query, key).reshape(heads, pick_count, total) * scale
        weights = jnp.where(same_doc[None], jnp.exp(jnp.where(same_doc[None], scores, -1e30)), 0.0)
        prob = weights / jnp.sum(weights, axis=2, keepdims=True)
        prob_b = prob.astype(BF).reshape(heads * pick_count, total)
        mixes.append(collapse(mm(prob_b, value), head_mask, pick_count).astype(BF))
        state.append((query, key, value, prob, prob_b))
    first = jnp.where(half == 0, mixes[0], mixes[1])
    second = jnp.where(half == 0, mixes[1], mixes[0])
    attn_out = mm(jnp.concatenate([first, second], axis=1), out_full)

    vec = picked_rows.astype(F32) + attn_out
    inv = lax.rsqrt(jnp.sum(vec * vec, axis=1, keepdims=True) + EPSILON)
    unit = vec * inv
    all_emb = lax.all_gather(unit.astype(BF), "dp", axis=0)
    all_fig = all_emb[:, :pair_count].reshape(-1, width)
    all_cap = all_emb[:, pair_count:].reshape(-1, width)
    logit_mult = logit_scale[0]
    logits = logit_mult * mmt(all_fig, all_cap)
    row_lse = jnp.log(jnp.sum(jnp.exp(logits), axis=1))
    col_lse = jnp.log(jnp.sum(jnp.exp(logits), axis=0))
    group_pairs = logits.shape[0]
    eye = jnp.arange(group_pairs)[:, None] == jnp.arange(group_pairs)[None, :]
    diag = jnp.sum(jnp.where(eye, logits, 0.0), axis=1)
    eye = eye.astype(F32)
    all_loss = 0.5 * (row_lse - diag) + 0.5 * (col_lse - diag)
    pair_loss = lax.dynamic_slice_in_dim(all_loss, me * pair_count, pair_count, 0)
    coef = 0.5 * group_ct[:, None] * (jnp.exp(logits - row_lse[:, None]) - eye) + 0.5 * (
        jnp.exp(logits - col_lse[None, :]) - eye
    ) * group_ct[None, :]
    coef_f = lax.dynamic_slice_in_dim(coef, me * pair_count, pair_count, 0)
    coef_c = lax.dynamic_slice_in_dim(coef.T, me * pair_count, pair_count, 0)
    grad = logit_mult * jnp.concatenate(
        [exact_mm(coef_f, all_cap), exact_mm(coef_c, all_fig)], axis=0
    )
    dvec = inv * (grad - unit * jnp.sum(unit * grad, axis=1, keepdims=True))

    dmix = mmt(dvec.astype(BF), out_full).astype(BF)
    low, high = dmix[:, :half_width], dmix[:, half_width:]
    dmix_m = jnp.where(half == 0, low, high)
    dmix_o = jnp.where(half == 0, high, low)
    row_ct = 0.0
    picked_ct = dvec
    for (query, key, value, prob, prob_b), w_q, w_k, w_v, dmix_h in (
        (state[0], query_m, key_m, value_m, dmix_m),
        (state[1], query_o, key_o, value_o, dmix_o),
    ):
        dmix_e = expand(dmix_h, head_mask)
        dprob = mmt(dmix_e, value).reshape(heads, pick_count, total)
        dscore = prob * (dprob - jnp.sum(dprob * prob, axis=2, keepdims=True)) * scale
        dscore = dscore.astype(BF).reshape(heads * pick_count, total)
        dquery = collapse(mm(dscore, key), head_mask, pick_count).astype(BF)
        dkey = tmm(dscore, query).astype(BF)
        dvalue = tmm(prob_b, dmix_e).astype(BF)
        row_ct = row_ct + mmt(dkey, w_k) + mmt(dvalue, w_v)
        picked_ct = picked_ct + mmt(dquery, w_q)
    ct_hi = picked_ct.astype(BF)
    ct_lo = (picked_ct - ct_hi.astype(F32)).astype(BF)
    row_ct = row_ct + tmm(
        jnp.concatenate([picked, picked], axis=0), jnp.concatenate([ct_hi, ct_lo], axis=0)
    )
    home = lax.all_to_all(row_ct.astype(BF), "dp", split_axis=0, concat_axis=0, tiled=True)
    page_grad = tmm(place.astype(BF), home).astype(BF)
    return (page_grad, pair_loss)


def solution(mesh):
    return jax.shard_map(
        body,
        mesh=mesh,
        in_specs=(
            P(("dp", "fsdp"), None),
            P(("dp", "fsdp")),
            P(("dp", "fsdp"), None),
            P(None, "fsdp", None),
            P(None, "fsdp"),
            P(("dp", "fsdp")),
            P(("dp", "fsdp")),
            P(),
            P(("dp", "fsdp")),
        ),
        out_specs=(P(("dp", "fsdp"), None), P(("dp", "fsdp"))),
        check_vma=False,
    )
```

```python
import functools
import math

import jax
import jax.numpy as jnp
from jax import lax
from jax.experimental import pallas as pl
from jax.experimental.pallas import tpu as pltpu
from jax.sharding import PartitionSpec as P

HD = 64
EPSILON = 1e-06
FIXED = 2.0**20
BF = jnp.bfloat16
F32 = jnp.float32


def mm(a, b):
    return jnp.dot(a, b, preferred_element_type=F32)


def mmt(a, b):
    return lax.dot_general(a, b, (((1,), (1,)), ((), ())), preferred_element_type=F32)


def tmm(a, b):
    return lax.dot_general(a, b, (((0,), (0,)), ((), ())), preferred_element_type=F32)


def split3(x):
    hi = x.astype(BF)
    rest = x - hi.astype(F32)
    mid = rest.astype(BF)
    low = (rest - mid.astype(F32)).astype(BF)
    return jnp.concatenate([hi, mid, low], axis=0)


def exact_mm(x, emb):
    count = x.shape[0]
    parts = mm(split3(x), emb)
    return parts[:count] + parts[count : 2 * count] + parts[2 * count :]


def expand(x, head_mask):
    return (x[None] * head_mask.astype(x.dtype)).reshape(-1, x.shape[1])


def collapse(x, head_mask, rows):
    return jnp.sum(x.reshape(-1, rows, x.shape[1]) * head_mask, axis=0)


def move_kernel(
    dp_count,
    fs_count,
    capacity,
    rows_ref,
    qkv_ref,
    out_w_ref,
    got_ref,
    wq_ref,
    wkv_ref,
    wo_ref,
    z_send,
    z_recv,
    xy_send,
    xy_recv,
    sib_send,
    sib_recv,
    page_send,
    page_recv,
    local_sem,
):
    d = lax.axis_index("dp")
    f = lax.axis_index("fsdp")
    depth = qkv_ref.shape[1]
    hdim = qkv_ref.shape[2]
    cut = out_w_ref.shape[1]
    parity = d % 2
    chip = d // 2
    chips = dp_count // 2
    sibling = d + 1 - 2 * parity
    half_rows = depth // 2
    piece_rows = depth // dp_count
    half_out = hdim // 2
    piece_out = hdim // dp_count

    def put(src, dst, send, recv, dp, fsdp):
        return pltpu.make_async_remote_copy(
            src_ref=src,
            dst_ref=dst,
            send_sem=send,
            recv_sem=recv,
            device_id=(dp, fsdp),
            device_id_type=pl.DeviceIdType.MESH,
        )

    def at(owner, start, count):
        return pl.ds(pl.multiple_of(owner * depth + start, 16), count)

    def wo_at(owner, start, count):
        return wo_ref.at[
            pl.ds(pl.multiple_of(start, 16), count), pl.ds(pl.multiple_of(owner * cut, 128), cut)
        ]

    def regions(owner, c, piece):
        half = at(owner, c * half_rows, half_rows)
        small = at(owner, c * half_rows + piece * piece_rows, piece_rows)
        return dict(
            q=wq_ref.at[half, :],
            k=wkv_ref.at[half, pl.ds(0, hdim)],
            v=wkv_ref.at[small, pl.ds(hdim, hdim)],
            o=wo_at(owner, c * half_out + piece * piece_out, piece_out),
            v_half=wkv_ref.at[half, pl.ds(hdim, hdim)],
            o_half=wo_at(owner, c * half_out, half_out),
        )

    barrier = pltpu.get_barrier_semaphore()
    for k in range(1, fs_count):
        pl.semaphore_signal(
            barrier, inc=1, device_id=(d, (f + k) % fs_count), device_id_type=pl.DeviceIdType.MESH
        )
    for k in range(1, dp_count):
        pl.semaphore_signal(
            barrier, inc=1, device_id=((d + k) % dp_count, f), device_id_type=pl.DeviceIdType.MESH
        )
    pl.semaphore_wait(barrier, fs_count + dp_count - 2)

    sends = []

    def begin(copy):
        copy.start()
        sends.append(copy)

    half_src = pl.ds(pl.multiple_of(parity * half_rows, 16), half_rows)
    piece_src = pl.ds(
        pl.multiple_of(parity * half_rows + chip * piece_rows, 16), piece_rows
    )
    out_src = pl.ds(pl.multiple_of(parity * half_out + chip * piece_out, 16), piece_out)
    sources = dict(
        q=qkv_ref.at[0, half_src, :],
        k=qkv_ref.at[1, half_src, :],
        v=qkv_ref.at[2, piece_src, :],
        o=out_w_ref.at[out_src, :],
    )
    mine = regions(f, parity, chip)
    names = ("v", "o", "k", "q")
    for i, name in enumerate(names):
        for k in range(1, fs_count):
            begin(put(sources[name], mine[name], z_send.at[i, k], z_recv.at[i, k],
                      d, (f + k) % fs_count))
    for k in range(1, dp_count):
        to = (d + k) % dp_count
        begin(put(rows_ref.at[pl.ds(pl.multiple_of(to * capacity, 8), capacity), :],
                  got_ref.at[pl.ds(pl.multiple_of(d * capacity, 8), capacity), :],
                  page_send.at[k], page_recv.at[k], to, f))
    own = pl.ds(pl.multiple_of(d * capacity, 8), capacity)
    whole = at(f, 0, depth)
    locals_ = [
        pltpu.make_async_copy(rows_ref.at[own, :], got_ref.at[own, :], local_sem.at[0]),
        pltpu.make_async_copy(qkv_ref.at[0], wq_ref.at[whole, :], local_sem.at[1]),
        pltpu.make_async_copy(qkv_ref.at[1], wkv_ref.at[whole, pl.ds(0, hdim)], local_sem.at[2]),
        pltpu.make_async_copy(qkv_ref.at[2], wkv_ref.at[whole, pl.ds(hdim, hdim)], local_sem.at[3]),
        pltpu.make_async_copy(out_w_ref, wo_at(f, 0, hdim), local_sem.at[4]),
    ]
    for copy in locals_:
        copy.start()

    def arrived(region, send, recv):
        put(region, region, send, recv, sibling, f).wait_recv()

    for i, name in enumerate(("v", "o")):
        for k in range(1, fs_count):
            owner = (f + fs_count - k) % fs_count
            place = regions(owner, parity, chip)[name]
            arrived(place, z_send.at[i, k], z_recv.at[i, k])
            for j in range(1, chips):
                begin(put(place, place, xy_send.at[i, k, j], xy_recv.at[i, k, j],
                          2 * ((chip + j) % chips) + parity, f))
    for i, name in ((0, "v"), (1, "o"), (2, "k"), (3, "q")):
        for k in range(1, fs_count):
            owner = (f + fs_count - k) % fs_count
            if i < 2:
                for j in range(1, chips):
                    origin = (chip + chips - j) % chips
                    arrived(regions(owner, parity, origin)[name],
                            xy_send.at[i, k, j], xy_recv.at[i, k, j])
                place = regions(owner, parity, 0)[name + "_half"]
            else:
                place = regions(owner, parity, 0)[name]
                arrived(place, z_send.at[i, k], z_recv.at[i, k])
            begin(put(place, place, sib_send.at[i, k], sib_recv.at[i, k], sibling, f))
    for k in range(1, dp_count):
        origin = (d + dp_count - k) % dp_count
        arrived(got_ref.at[pl.ds(pl.multiple_of(origin * capacity, 8), capacity), :],
                page_send.at[k], page_recv.at[k])
    for i, name in ((0, "v_half"), (1, "o_half"), (2, "k"), (3, "q")):
        for k in range(1, fs_count):
            owner = (f + fs_count - k) % fs_count
            arrived(regions(owner, 1 - parity, 0)[name], sib_send.at[i, k], sib_recv.at[i, k])
    for copy in locals_:
        copy.wait()
    for copy in sends:
        copy.wait_send()


def move(send_rows, qkv_weight, out_weight, dp_count, fs_count, capacity):
    _, depth, hdim = qkv_weight.shape
    width = send_rows.shape[1]
    sem = pltpu.SemaphoreType.DMA
    any_spec = pl.BlockSpec(memory_space=pl.ANY)
    return pl.pallas_call(
        functools.partial(move_kernel, dp_count, fs_count, capacity),
        out_shape=(
            jax.ShapeDtypeStruct(send_rows.shape, BF),
            jax.ShapeDtypeStruct((depth * fs_count, hdim), BF),
            jax.ShapeDtypeStruct((depth * fs_count, 2 * hdim), BF),
            jax.ShapeDtypeStruct((hdim, width), BF),
        ),
        in_specs=[any_spec] * 3,
        out_specs=(any_spec,) * 4,
        scratch_shapes=[
            sem((4, fs_count)),
            sem((4, fs_count)),
            sem((2, fs_count, dp_count // 2)),
            sem((2, fs_count, dp_count // 2)),
            sem((4, fs_count)),
            sem((4, fs_count)),
            sem((dp_count,)),
            sem((dp_count,)),
            sem((5,)),
        ],
        compiler_params=pltpu.CompilerParams(collective_id=0, has_side_effects=True),
    )(send_rows, qkv_weight, out_weight)


def body(
    page_embed,
    page_slot,
    doc_ids,
    qkv_weight,
    out_weight,
    fig_slot,
    cap_slot,
    logit_scale,
    loss_cotangent,
):
    dp_count = lax.axis_size("dp")
    me = lax.axis_index("dp")
    fs_count = lax.axis_size("fsdp")
    row_count, width = page_embed.shape
    capacity = -(-(5 * row_count) // (4 * dp_count))
    capacity = -(-capacity // 16) * 16
    total = dp_count * capacity
    pair_count = fig_slot.shape[0]
    hdim = qkv_weight.shape[2]
    owner_idx = page_slot // row_count
    slot_idx = page_slot % row_count
    onehot = (owner_idx[:, None] == jnp.arange(dp_count)[None, :]).astype(jnp.int32)
    rank_idx = jnp.sum((jnp.cumsum(onehot, axis=0) - onehot) * onehot, axis=1)
    place_idx = owner_idx * capacity + rank_idx
    place = jnp.arange(total)[:, None] == place_idx[None, :]
    send_ids = jnp.sum(jnp.where(place, slot_idx[None, :] + 1, 0), axis=1) - 1
    fixed_ct = (loss_cotangent * FIXED).astype(jnp.int32)
    send_ints = jnp.concatenate(
        [
            send_ids.reshape(dp_count, capacity),
            jnp.broadcast_to(fixed_ct[None, :], (dp_count, pair_count)),
        ],
        axis=1,
    )
    recv_ints = lax.all_to_all(send_ints, "dp", split_axis=0, concat_axis=0, tiled=True)
    send_rows = mm(place.astype(BF), page_embed).astype(BF)
    rows, w_q, w_kv, w_out = move(
        send_rows, qkv_weight, out_weight, dp_count, fs_count, capacity
    )

    ids = recv_ints[:, :capacity].reshape(-1)
    group_ct = recv_ints[:, capacity:].reshape(-1).astype(F32) * (1.0 / FIXED)
    doc_row = doc_ids[0]
    slot_range = jnp.arange(row_count)
    row_docs = (
        jnp.sum(jnp.where(ids[:, None] == slot_range[None, :], doc_row[None, :] + 1, 0), axis=1) - 1
    )
    slots = jnp.concatenate([fig_slot, cap_slot])
    slot_docs = jnp.sum(jnp.where(slots[:, None] == slot_range[None, :], doc_row[None, :], 0), axis=1)
    picked = (slots[:, None] == ids[None, :]).astype(BF)
    same_doc = slot_docs[:, None] == row_docs[None, :]
    pick_count = slots.shape[0]

    picked_rows = mm(picked, rows).astype(BF)
    scale = 1.0 / math.sqrt(HD)
    heads = hdim // HD
    head_mask = (
        jnp.arange(hdim)[None, None, :] // HD == jnp.arange(heads)[:, None, None]
    ).astype(F32)

    key_value = mm(rows, w_kv).astype(BF)
    key, value = key_value[:, :hdim], key_value[:, hdim:]
    query = expand(mm(picked_rows, w_q).astype(BF), head_mask)
    scores = mmt(query, key).reshape(heads, pick_count, total) * scale
    weights = jnp.exp(jnp.where(same_doc[None], scores, -1e30))
    prob = weights / jnp.sum(weights, axis=2, keepdims=True)
    prob_b = prob.astype(BF).reshape(heads * pick_count, total)
    mixed = collapse(mm(prob_b, value), head_mask, pick_count).astype(BF)
    attn_out = mm(mixed, w_out)

    vec = picked_rows.astype(F32) + attn_out
    inv = lax.rsqrt(jnp.sum(vec * vec, axis=1, keepdims=True) + EPSILON)
    unit = vec * inv
    all_fig = lax.all_gather(unit[:pair_count].astype(BF), "dp", axis=0, tiled=True)
    all_cap = lax.all_gather(unit[pair_count:].astype(BF), "dp", axis=0, tiled=True)
    logit_mult = logit_scale[0]
    logits = logit_mult * mmt(all_fig, all_cap)
    row_lse = jnp.log(jnp.sum(jnp.exp(logits), axis=1))
    col_lse = jnp.log(jnp.sum(jnp.exp(logits), axis=0))
    group_pairs = logits.shape[0]
    eye = jnp.arange(group_pairs)[:, None] == jnp.arange(group_pairs)[None, :]
    diag = jnp.sum(jnp.where(eye, logits, 0.0), axis=1)
    eye = eye.astype(F32)
    all_loss = 0.5 * (row_lse - diag) + 0.5 * (col_lse - diag)
    pair_loss = lax.dynamic_slice_in_dim(all_loss, me * pair_count, pair_count, 0)
    coef = 0.5 * group_ct[:, None] * (jnp.exp(logits - row_lse[:, None]) - eye) + 0.5 * (
        jnp.exp(logits - col_lse[None, :]) - eye
    ) * group_ct[None, :]
    coef_f = lax.dynamic_slice_in_dim(coef, me * pair_count, pair_count, 0)
    coef_c = lax.dynamic_slice_in_dim(coef.T, me * pair_count, pair_count, 0)
    grad = logit_mult * jnp.concatenate(
        [exact_mm(coef_f, all_cap), exact_mm(coef_c, all_fig)], axis=0
    )
    dvec = inv * (grad - unit * jnp.sum(unit * grad, axis=1, keepdims=True))

    dmix = expand(mmt(dvec.astype(BF), w_out).astype(BF), head_mask)
    dprob = mmt(dmix, value).reshape(heads, pick_count, total)
    dscore = prob * (dprob - jnp.sum(dprob * prob, axis=2, keepdims=True)) * scale
    dscore = dscore.astype(BF).reshape(heads * pick_count, total)
    dquery = collapse(mm(dscore, key), head_mask, pick_count).astype(BF)
    picked_ct = dvec + mmt(dquery, w_q)
    dkey_value = jnp.concatenate(
        [tmm(dscore, query).astype(BF), tmm(prob_b, dmix).astype(BF)], axis=1
    )
    ct_hi = picked_ct.astype(BF)
    ct_lo = (picked_ct - ct_hi.astype(F32)).astype(BF)
    row_ct = mmt(dkey_value, w_kv) + tmm(
        jnp.concatenate([picked, picked], axis=0), jnp.concatenate([ct_hi, ct_lo], axis=0)
    )
    home = lax.all_to_all(row_ct.astype(BF), "dp", split_axis=0, concat_axis=0, tiled=True)
    page_grad = tmm(place.astype(BF), home).astype(BF)
    return (page_grad, pair_loss)


def solution(mesh):
    return jax.shard_map(
        body,
        mesh=mesh,
        in_specs=(
            P(("dp", "fsdp"), None),
            P(("dp", "fsdp")),
            P(("dp", "fsdp"), None),
            P(None, "fsdp", None),
            P(None, "fsdp"),
            P(("dp", "fsdp")),
            P(("dp", "fsdp")),
            P(),
            P(("dp", "fsdp")),
        ),
        out_specs=(P(("dp", "fsdp"), None), P(("dp", "fsdp"))),
        check_vma=False,
    )
```

```python
import functools
import math

import jax
import jax.numpy as jnp
from jax import lax
from jax.experimental import pallas as pl
from jax.experimental.pallas import tpu as pltpu
from jax.sharding import PartitionSpec as P

HD = 64
EPSILON = 1e-06
FIXED = 2.0**20
BF = jnp.bfloat16
F32 = jnp.float32


def mm(a, b):
    return jnp.dot(a, b, preferred_element_type=F32)


def mmt(a, b):
    return lax.dot_general(a, b, (((1,), (1,)), ((), ())), preferred_element_type=F32)


def tmm(a, b):
    return lax.dot_general(a, b, (((0,), (0,)), ((), ())), preferred_element_type=F32)


def split3(x):
    hi = x.astype(BF)
    rest = x - hi.astype(F32)
    mid = rest.astype(BF)
    low = (rest - mid.astype(F32)).astype(BF)
    return jnp.concatenate([hi, mid, low], axis=0)


def exact_mm(x, emb):
    count = x.shape[0]
    parts = mm(split3(x), emb)
    return parts[:count] + parts[count : 2 * count] + parts[2 * count :]


def expand(x, head_mask):
    return (x[None] * head_mask.astype(x.dtype)).reshape(-1, x.shape[1])


def collapse(x, head_mask, rows):
    return jnp.sum(x.reshape(-1, rows, x.shape[1]) * head_mask, axis=0)


def move_kernel(
    dp_count,
    fs_count,
    capacity,
    rows_ref,
    qkv_ref,
    out_w_ref,
    ints_ref,
    got_ref,
    wq_ref,
    wkv_ref,
    wo_ref,
    got_ints_ref,
    z_send,
    z_recv,
    xy_send,
    xy_recv,
    sib_send,
    sib_recv,
    page_send,
    page_recv,
    ints_send,
    ints_recv,
    local_sem,
):
    d = lax.axis_index("dp")
    f = lax.axis_index("fsdp")
    depth = qkv_ref.shape[1]
    hdim = qkv_ref.shape[2]
    cut = out_w_ref.shape[1]
    parity = d % 2
    chip = d // 2
    chips = dp_count // 2
    sibling = d + 1 - 2 * parity
    half_rows = depth // 2
    piece_rows = depth // dp_count
    half_out = hdim // 2
    piece_out = hdim // dp_count

    def put(src, dst, send, recv, dp, fsdp):
        return pltpu.make_async_remote_copy(
            src_ref=src,
            dst_ref=dst,
            send_sem=send,
            recv_sem=recv,
            device_id=(dp, fsdp),
            device_id_type=pl.DeviceIdType.MESH,
        )

    def at(owner, start, count):
        return pl.ds(pl.multiple_of(owner * depth + start, 16), count)

    def wo_at(owner, start, count):
        return wo_ref.at[
            pl.ds(pl.multiple_of(start, 16), count), pl.ds(pl.multiple_of(owner * cut, 128), cut)
        ]

    def regions(owner, c, piece):
        half = at(owner, c * half_rows, half_rows)
        small = at(owner, c * half_rows + piece * piece_rows, piece_rows)
        return dict(
            q=wq_ref.at[half, :],
            k=wkv_ref.at[small, pl.ds(0, hdim)],
            k_half=wkv_ref.at[half, pl.ds(0, hdim)],
            v=wkv_ref.at[small, pl.ds(hdim, hdim)],
            o=wo_at(owner, c * half_out + piece * piece_out, piece_out),
            v_half=wkv_ref.at[half, pl.ds(hdim, hdim)],
            o_half=wo_at(owner, c * half_out, half_out),
        )

    barrier = pltpu.get_barrier_semaphore()
    for k in range(1, fs_count):
        pl.semaphore_signal(
            barrier, inc=1, device_id=(d, (f + k) % fs_count), device_id_type=pl.DeviceIdType.MESH
        )
    for k in range(1, dp_count):
        pl.semaphore_signal(
            barrier, inc=1, device_id=((d + k) % dp_count, f), device_id_type=pl.DeviceIdType.MESH
        )
    pl.semaphore_wait(barrier, fs_count + dp_count - 2)

    sends = []

    def begin(copy):
        copy.start()
        sends.append(copy)

    half_src = pl.ds(pl.multiple_of(parity * half_rows, 16), half_rows)
    piece_src = pl.ds(
        pl.multiple_of(parity * half_rows + chip * piece_rows, 16), piece_rows
    )
    out_src = pl.ds(pl.multiple_of(parity * half_out + chip * piece_out, 16), piece_out)
    sources = dict(
        q=qkv_ref.at[0, half_src, :],
        k=qkv_ref.at[1, piece_src, :],
        v=qkv_ref.at[2, piece_src, :],
        o=out_w_ref.at[out_src, :],
    )
    mine = regions(f, parity, chip)
    names = ("k", "v", "o", "q")
    for i, name in enumerate(names):
        for k in range(1, fs_count):
            begin(put(sources[name], mine[name], z_send.at[i, k], z_recv.at[i, k],
                      d, (f + k) % fs_count))
    for k in range(1, dp_count):
        to = (d + k) % dp_count
        begin(put(rows_ref.at[pl.ds(pl.multiple_of(to * capacity, 8), capacity), :],
                  got_ref.at[pl.ds(pl.multiple_of(d * capacity, 8), capacity), :],
                  page_send.at[k], page_recv.at[k], to, f))
        begin(put(ints_ref.at[to], got_ints_ref.at[d], ints_send.at[k], ints_recv.at[k], to, f))
    own = pl.ds(pl.multiple_of(d * capacity, 8), capacity)
    whole = at(f, 0, depth)
    locals_ = [
        pltpu.make_async_copy(rows_ref.at[own, :], got_ref.at[own, :], local_sem.at[0]),
        pltpu.make_async_copy(qkv_ref.at[0], wq_ref.at[whole, :], local_sem.at[1]),
        pltpu.make_async_copy(qkv_ref.at[1], wkv_ref.at[whole, pl.ds(0, hdim)], local_sem.at[2]),
        pltpu.make_async_copy(qkv_ref.at[2], wkv_ref.at[whole, pl.ds(hdim, hdim)], local_sem.at[3]),
        pltpu.make_async_copy(out_w_ref, wo_at(f, 0, hdim), local_sem.at[4]),
        pltpu.make_async_copy(ints_ref.at[d], got_ints_ref.at[d], local_sem.at[5]),
    ]
    for copy in locals_:
        copy.start()

    def arrived(region, send, recv):
        put(region, region, send, recv, sibling, f).wait_recv()

    for i, name in enumerate(names[:3]):
        for k in range(1, fs_count):
            owner = (f + fs_count - k) % fs_count
            place = regions(owner, parity, chip)[name]
            arrived(place, z_send.at[i, k], z_recv.at[i, k])
            for j in range(1, chips):
                begin(put(place, place, xy_send.at[i, k, j], xy_recv.at[i, k, j],
                          2 * ((chip + j) % chips) + parity, f))
    for i, name in enumerate(names):
        for k in range(1, fs_count):
            owner = (f + fs_count - k) % fs_count
            if i < 3:
                for j in range(1, chips):
                    origin = (chip + chips - j) % chips
                    arrived(regions(owner, parity, origin)[name],
                            xy_send.at[i, k, j], xy_recv.at[i, k, j])
                place = regions(owner, parity, 0)[name + "_half"]
            else:
                place = regions(owner, parity, 0)[name]
                arrived(place, z_send.at[i, k], z_recv.at[i, k])
            begin(put(place, place, sib_send.at[i, k], sib_recv.at[i, k], sibling, f))
    for k in range(1, dp_count):
        origin = (d + dp_count - k) % dp_count
        arrived(got_ref.at[pl.ds(pl.multiple_of(origin * capacity, 8), capacity), :],
                page_send.at[k], page_recv.at[k])
        arrived(got_ints_ref.at[origin], ints_send.at[k], ints_recv.at[k])
    for i, name in enumerate(("k_half", "v_half", "o_half", "q")):
        for k in range(1, fs_count):
            owner = (f + fs_count - k) % fs_count
            arrived(regions(owner, 1 - parity, 0)[name], sib_send.at[i, k], sib_recv.at[i, k])
    for copy in locals_:
        copy.wait()
    for copy in sends:
        copy.wait_send()


def move(send_rows, qkv_weight, out_weight, ints, dp_count, fs_count, capacity):
    _, depth, hdim = qkv_weight.shape
    width = send_rows.shape[1]
    sem = pltpu.SemaphoreType.DMA
    any_spec = pl.BlockSpec(memory_space=pl.ANY)
    return pl.pallas_call(
        functools.partial(move_kernel, dp_count, fs_count, capacity),
        out_shape=(
            jax.ShapeDtypeStruct(send_rows.shape, BF),
            jax.ShapeDtypeStruct((depth * fs_count, hdim), BF),
            jax.ShapeDtypeStruct((depth * fs_count, 2 * hdim), BF),
            jax.ShapeDtypeStruct((hdim, width), BF),
            jax.ShapeDtypeStruct(ints.shape, jnp.int32),
        ),
        in_specs=[any_spec] * 4,
        out_specs=(any_spec,) * 5,
        scratch_shapes=[
            sem((4, fs_count)),
            sem((4, fs_count)),
            sem((3, fs_count, dp_count // 2)),
            sem((3, fs_count, dp_count // 2)),
            sem((4, fs_count)),
            sem((4, fs_count)),
            sem((dp_count,)),
            sem((dp_count,)),
            sem((dp_count,)),
            sem((dp_count,)),
            sem((6,)),
        ],
        compiler_params=pltpu.CompilerParams(collective_id=0, has_side_effects=True),
    )(send_rows, qkv_weight, out_weight, ints)


def share_kernel(dp_count, emb_ref, all_ref, send, recv):
    d = lax.axis_index("dp")
    f = lax.axis_index("fsdp")
    barrier = pltpu.get_barrier_semaphore()
    for k in range(1, dp_count):
        pl.semaphore_signal(
            barrier, inc=1, device_id=((d + k) % dp_count, f), device_id_type=pl.DeviceIdType.MESH
        )
    pl.semaphore_wait(barrier, dp_count - 1)

    def put(place, k, to):
        return pltpu.make_async_remote_copy(
            src_ref=emb_ref,
            dst_ref=all_ref.at[place],
            send_sem=send.at[k],
            recv_sem=recv.at[k],
            device_id=(to, f),
            device_id_type=pl.DeviceIdType.MESH,
        )

    copies = [put(d, k, (d + k) % dp_count) for k in range(1, dp_count)]
    for copy in copies:
        copy.start()
    all_ref[d] = emb_ref[...]
    for k in range(1, dp_count):
        put((d + dp_count - k) % dp_count, k, (d + k) % dp_count).wait_recv()
    for copy in copies:
        copy.wait_send()


def share(emb, dp_count):
    return pl.pallas_call(
        functools.partial(share_kernel, dp_count),
        out_shape=jax.ShapeDtypeStruct((dp_count,) + emb.shape, emb.dtype),
        in_specs=[pl.BlockSpec(memory_space=pltpu.VMEM)],
        out_specs=pl.BlockSpec(memory_space=pltpu.VMEM),
        scratch_shapes=[pltpu.SemaphoreType.DMA((dp_count,)), pltpu.SemaphoreType.DMA((dp_count,))],
        compiler_params=pltpu.CompilerParams(collective_id=1, has_side_effects=True),
    )(emb)


def body(
    page_embed,
    page_slot,
    doc_ids,
    qkv_weight,
    out_weight,
    fig_slot,
    cap_slot,
    logit_scale,
    loss_cotangent,
):
    dp_count = lax.axis_size("dp")
    me = lax.axis_index("dp")
    fs_count = lax.axis_size("fsdp")
    row_count, width = page_embed.shape
    capacity = -(-(5 * row_count) // (4 * dp_count))
    capacity = -(-capacity // 16) * 16
    total = dp_count * capacity
    pair_count = fig_slot.shape[0]
    hdim = qkv_weight.shape[2]
    owner_idx = page_slot // row_count
    slot_idx = page_slot % row_count
    onehot = (owner_idx[:, None] == jnp.arange(dp_count)[None, :]).astype(jnp.int32)
    rank_idx = jnp.sum((jnp.cumsum(onehot, axis=0) - onehot) * onehot, axis=1)
    place_idx = owner_idx * capacity + rank_idx
    place = jnp.arange(total)[:, None] == place_idx[None, :]
    send_ids = jnp.sum(jnp.where(place, slot_idx[None, :] + 1, 0), axis=1) - 1
    fixed_ct = (loss_cotangent * FIXED).astype(jnp.int32)
    send_ints = jnp.concatenate(
        [
            send_ids.reshape(dp_count, capacity),
            jnp.broadcast_to(fixed_ct[None, :], (dp_count, pair_count)),
        ],
        axis=1,
    )
    send_ints = jnp.pad(send_ints, ((0, 0), (0, -send_ints.shape[1] % 128)))
    send_ints = jnp.broadcast_to(send_ints[:, None], (dp_count, 8, send_ints.shape[1]))
    send_rows = mm(place.astype(BF), page_embed).astype(BF)
    rows, w_q, w_kv, w_out, recv_ints = move(
        send_rows, qkv_weight, out_weight, send_ints, dp_count, fs_count, capacity
    )
    recv_ints = recv_ints[:, 0]

    ids = recv_ints[:, :capacity].reshape(-1)
    group_ct = recv_ints[:, capacity : capacity + pair_count].reshape(-1).astype(F32) * (1.0 / FIXED)
    doc_row = doc_ids[0]
    slot_range = jnp.arange(row_count)
    row_docs = (
        jnp.sum(jnp.where(ids[:, None] == slot_range[None, :], doc_row[None, :] + 1, 0), axis=1) - 1
    )
    slots = jnp.concatenate([fig_slot, cap_slot])
    slot_docs = jnp.sum(jnp.where(slots[:, None] == slot_range[None, :], doc_row[None, :], 0), axis=1)
    picked = (slots[:, None] == ids[None, :]).astype(BF)
    same_doc = slot_docs[:, None] == row_docs[None, :]
    pick_count = slots.shape[0]

    picked_rows = mm(picked, rows).astype(BF)
    scale = 1.0 / math.sqrt(HD)
    heads = hdim // HD
    head_mask = (
        jnp.arange(hdim)[None, None, :] // HD == jnp.arange(heads)[:, None, None]
    ).astype(F32)

    key_value = mm(rows, w_kv).astype(BF)
    key, value = key_value[:, :hdim], key_value[:, hdim:]
    query = expand(mm(picked_rows, w_q).astype(BF), head_mask)
    scores = mmt(query, key).reshape(heads, pick_count, total) * scale
    weights = jnp.exp(jnp.where(same_doc[None], scores, -1e30))
    prob = weights / jnp.sum(weights, axis=2, keepdims=True)
    prob_b = prob.astype(BF).reshape(heads * pick_count, total)
    mixed = collapse(mm(prob_b, value), head_mask, pick_count).astype(BF)
    attn_out = mm(mixed, w_out)

    vec = picked_rows.astype(F32) + attn_out
    inv = lax.rsqrt(jnp.sum(vec * vec, axis=1, keepdims=True) + EPSILON)
    unit = vec * inv
    all_emb = share(unit.astype(BF), dp_count)
    all_fig = all_emb[:, :pair_count].reshape(-1, width)
    all_cap = all_emb[:, pair_count:].reshape(-1, width)
    logit_mult = logit_scale[0]
    logits = logit_mult * mmt(all_fig, all_cap)
    row_lse = jnp.log(jnp.sum(jnp.exp(logits), axis=1))
    col_lse = jnp.log(jnp.sum(jnp.exp(logits), axis=0))
    group_pairs = logits.shape[0]
    eye = jnp.arange(group_pairs)[:, None] == jnp.arange(group_pairs)[None, :]
    diag = jnp.sum(jnp.where(eye, logits, 0.0), axis=1)
    eye = eye.astype(F32)
    all_loss = 0.5 * (row_lse - diag) + 0.5 * (col_lse - diag)
    pair_loss = lax.dynamic_slice_in_dim(all_loss, me * pair_count, pair_count, 0)
    coef = 0.5 * group_ct[:, None] * (jnp.exp(logits - row_lse[:, None]) - eye) + 0.5 * (
        jnp.exp(logits - col_lse[None, :]) - eye
    ) * group_ct[None, :]
    coef_f = lax.dynamic_slice_in_dim(coef, me * pair_count, pair_count, 0)
    coef_c = lax.dynamic_slice_in_dim(coef.T, me * pair_count, pair_count, 0)
    grad = logit_mult * jnp.concatenate(
        [exact_mm(coef_f, all_cap), exact_mm(coef_c, all_fig)], axis=0
    )
    dvec = inv * (grad - unit * jnp.sum(unit * grad, axis=1, keepdims=True))

    dmix = expand(mmt(dvec.astype(BF), w_out).astype(BF), head_mask)
    dprob = mmt(dmix, value).reshape(heads, pick_count, total)
    dscore = prob * (dprob - jnp.sum(dprob * prob, axis=2, keepdims=True)) * scale
    dscore = dscore.astype(BF).reshape(heads * pick_count, total)
    dquery = collapse(mm(dscore, key), head_mask, pick_count).astype(BF)
    picked_ct = dvec + mmt(dquery, w_q)
    dkey_value = jnp.concatenate(
        [tmm(dscore, query).astype(BF), tmm(prob_b, dmix).astype(BF)], axis=1
    )
    ct_hi = picked_ct.astype(BF)
    ct_lo = (picked_ct - ct_hi.astype(F32)).astype(BF)
    row_ct = mmt(dkey_value, w_kv) + tmm(
        jnp.concatenate([picked, picked], axis=0), jnp.concatenate([ct_hi, ct_lo], axis=0)
    )
    home = lax.all_to_all(row_ct.astype(BF), "dp", split_axis=0, concat_axis=0, tiled=True)
    page_grad = tmm(place.astype(BF), home).astype(BF)
    return (page_grad, pair_loss)


def solution(mesh):
    return jax.shard_map(
        body,
        mesh=mesh,
        in_specs=(
            P(("dp", "fsdp"), None),
            P(("dp", "fsdp")),
            P(("dp", "fsdp"), None),
            P(None, "fsdp", None),
            P(None, "fsdp"),
            P(("dp", "fsdp")),
            P(("dp", "fsdp")),
            P(),
            P(("dp", "fsdp")),
        ),
        out_specs=(P(("dp", "fsdp"), None), P(("dp", "fsdp"))),
        check_vma=False,
    )
```

```python
import functools
import math

import jax
import jax.numpy as jnp
from jax import lax
from jax.experimental import pallas as pl
from jax.experimental.pallas import tpu as pltpu
from jax.sharding import PartitionSpec as P

HD = 64
EPSILON = 1e-06
FIXED = 2.0**20
BF = jnp.bfloat16
F32 = jnp.float32


def mm(a, b):
    return jnp.dot(a, b, preferred_element_type=F32)


def mmt(a, b):
    return lax.dot_general(a, b, (((1,), (1,)), ((), ())), preferred_element_type=F32)


def tmm(a, b):
    return lax.dot_general(a, b, (((0,), (0,)), ((), ())), preferred_element_type=F32)


def split3(x):
    hi = x.astype(BF)
    rest = x - hi.astype(F32)
    mid = rest.astype(BF)
    low = (rest - mid.astype(F32)).astype(BF)
    return jnp.concatenate([hi, mid, low], axis=0)


def exact_mm(x, emb):
    count = x.shape[0]
    parts = mm(split3(x), emb)
    return parts[:count] + parts[count : 2 * count] + parts[2 * count :]


def expand(x, head_mask):
    return (x[None] * head_mask.astype(x.dtype)).reshape(-1, x.shape[1])


def collapse(x, head_mask, rows):
    return jnp.sum(x.reshape(-1, rows, x.shape[1]) * head_mask, axis=0)


def move_kernel(
    dp_count,
    fs_count,
    capacity,
    rows_ref,
    qkv_ref,
    out_w_ref,
    ints_ref,
    got_ref,
    wq_ref,
    wkv_ref,
    wo_ref,
    got_ints_ref,
    z_send,
    z_recv,
    xy_send,
    xy_recv,
    sib_send,
    sib_recv,
    page_send,
    page_recv,
    ints_send,
    ints_recv,
    local_sem,
):
    d = lax.axis_index("dp")
    f = lax.axis_index("fsdp")
    depth = qkv_ref.shape[1]
    hdim = qkv_ref.shape[2]
    cut = out_w_ref.shape[1]
    parity = d % 2
    chip = d // 2
    chips = dp_count // 2
    sibling = d + 1 - 2 * parity
    half_rows = depth // 2
    piece_rows = depth // dp_count
    half_out = hdim // 2
    piece_out = hdim // dp_count

    def put(src, dst, send, recv, dp, fsdp):
        return pltpu.make_async_remote_copy(
            src_ref=src,
            dst_ref=dst,
            send_sem=send,
            recv_sem=recv,
            device_id=(dp, fsdp),
            device_id_type=pl.DeviceIdType.MESH,
        )

    def at(owner, start, count):
        return pl.ds(pl.multiple_of(owner * depth + start, 16), count)

    def wo_at(owner, start, count):
        return wo_ref.at[
            pl.ds(pl.multiple_of(start, 16), count), pl.ds(pl.multiple_of(owner * cut, 128), cut)
        ]

    def regions(owner, c, piece):
        half = at(owner, c * half_rows, half_rows)
        small = at(owner, c * half_rows + piece * piece_rows, piece_rows)
        return dict(
            q=wq_ref.at[half, :],
            k=wkv_ref.at[small, pl.ds(0, hdim)],
            k_half=wkv_ref.at[half, pl.ds(0, hdim)],
            v=wkv_ref.at[small, pl.ds(hdim, hdim)],
            o=wo_at(owner, c * half_out + piece * piece_out, piece_out),
            v_half=wkv_ref.at[half, pl.ds(hdim, hdim)],
            o_half=wo_at(owner, c * half_out, half_out),
        )

    barrier = pltpu.get_barrier_semaphore()
    for k in range(1, fs_count):
        pl.semaphore_signal(
            barrier, inc=1, device_id=(d, (f + k) % fs_count), device_id_type=pl.DeviceIdType.MESH
        )
    for k in range(1, dp_count):
        pl.semaphore_signal(
            barrier, inc=1, device_id=((d + k) % dp_count, f), device_id_type=pl.DeviceIdType.MESH
        )
    pl.semaphore_wait(barrier, fs_count + dp_count - 2)

    sends = []

    def begin(copy):
        copy.start()
        sends.append(copy)

    half_src = pl.ds(pl.multiple_of(parity * half_rows, 16), half_rows)
    piece_src = pl.ds(
        pl.multiple_of(parity * half_rows + chip * piece_rows, 16), piece_rows
    )
    out_src = pl.ds(pl.multiple_of(parity * half_out + chip * piece_out, 16), piece_out)
    sources = dict(
        q=qkv_ref.at[0, half_src, :],
        k=qkv_ref.at[1, piece_src, :],
        v=qkv_ref.at[2, piece_src, :],
        o=out_w_ref.at[out_src, :],
    )
    mine = regions(f, parity, chip)
    names = ("k", "v", "o", "q")

    def begin_z(i, name):
        for k in range(1, fs_count):
            begin(put(sources[name], mine[name], z_send.at[i, k], z_recv.at[i, k],
                      d, (f + k) % fs_count))

    for i in range(3):
        begin_z(i, names[i])
    for k in range(1, dp_count):
        to = (d + k) % dp_count
        begin(put(rows_ref.at[pl.ds(pl.multiple_of(to * capacity, 8), capacity), :],
                  got_ref.at[pl.ds(pl.multiple_of(d * capacity, 8), capacity), :],
                  page_send.at[k], page_recv.at[k], to, f))
        begin(put(ints_ref.at[to], got_ints_ref.at[d], ints_send.at[k], ints_recv.at[k], to, f))
    begin_z(3, names[3])
    own = pl.ds(pl.multiple_of(d * capacity, 8), capacity)
    whole = at(f, 0, depth)
    locals_ = [
        pltpu.make_async_copy(rows_ref.at[own, :], got_ref.at[own, :], local_sem.at[0]),
        pltpu.make_async_copy(qkv_ref.at[0], wq_ref.at[whole, :], local_sem.at[1]),
        pltpu.make_async_copy(qkv_ref.at[1], wkv_ref.at[whole, pl.ds(0, hdim)], local_sem.at[2]),
        pltpu.make_async_copy(qkv_ref.at[2], wkv_ref.at[whole, pl.ds(hdim, hdim)], local_sem.at[3]),
        pltpu.make_async_copy(out_w_ref, wo_at(f, 0, hdim), local_sem.at[4]),
        pltpu.make_async_copy(ints_ref.at[d], got_ints_ref.at[d], local_sem.at[5]),
    ]
    for copy in locals_:
        copy.start()

    def arrived(region, send, recv):
        put(region, region, send, recv, sibling, f).wait_recv()

    for i, name in enumerate(names[:3]):
        for k in range(1, fs_count):
            owner = (f + fs_count - k) % fs_count
            place = regions(owner, parity, chip)[name]
            arrived(place, z_send.at[i, k], z_recv.at[i, k])
            for j in range(1, chips):
                begin(put(place, place, xy_send.at[i, k, j], xy_recv.at[i, k, j],
                          2 * ((chip + j) % chips) + parity, f))
    for i, name in enumerate(names):
        for k in range(1, fs_count):
            owner = (f + fs_count - k) % fs_count
            if i < 3:
                for j in range(1, chips):
                    origin = (chip + chips - j) % chips
                    arrived(regions(owner, parity, origin)[name],
                            xy_send.at[i, k, j], xy_recv.at[i, k, j])
                place = regions(owner, parity, 0)[name + "_half"]
            else:
                place = regions(owner, parity, 0)[name]
                arrived(place, z_send.at[i, k], z_recv.at[i, k])
            begin(put(place, place, sib_send.at[i, k], sib_recv.at[i, k], sibling, f))
    for k in range(1, dp_count):
        origin = (d + dp_count - k) % dp_count
        arrived(got_ref.at[pl.ds(pl.multiple_of(origin * capacity, 8), capacity), :],
                page_send.at[k], page_recv.at[k])
        arrived(got_ints_ref.at[origin], ints_send.at[k], ints_recv.at[k])
    for i, name in enumerate(("k_half", "v_half", "o_half", "q")):
        for k in range(1, fs_count):
            owner = (f + fs_count - k) % fs_count
            arrived(regions(owner, 1 - parity, 0)[name], sib_send.at[i, k], sib_recv.at[i, k])
    for copy in locals_:
        copy.wait()
    for copy in sends:
        copy.wait_send()


def move(send_rows, qkv_weight, out_weight, ints, dp_count, fs_count, capacity):
    _, depth, hdim = qkv_weight.shape
    width = send_rows.shape[1]
    sem = pltpu.SemaphoreType.DMA
    any_spec = pl.BlockSpec(memory_space=pl.ANY)
    return pl.pallas_call(
        functools.partial(move_kernel, dp_count, fs_count, capacity),
        out_shape=(
            jax.ShapeDtypeStruct(send_rows.shape, BF),
            jax.ShapeDtypeStruct((depth * fs_count, hdim), BF),
            jax.ShapeDtypeStruct((depth * fs_count, 2 * hdim), BF),
            jax.ShapeDtypeStruct((hdim, width), BF),
            jax.ShapeDtypeStruct(ints.shape, jnp.int32),
        ),
        in_specs=[any_spec] * 4,
        out_specs=(any_spec,) * 5,
        scratch_shapes=[
            sem((4, fs_count)),
            sem((4, fs_count)),
            sem((3, fs_count, dp_count // 2)),
            sem((3, fs_count, dp_count // 2)),
            sem((4, fs_count)),
            sem((4, fs_count)),
            sem((dp_count,)),
            sem((dp_count,)),
            sem((dp_count,)),
            sem((dp_count,)),
            sem((6,)),
        ],
        compiler_params=pltpu.CompilerParams(collective_id=0, has_side_effects=True),
    )(send_rows, qkv_weight, out_weight, ints)


def share_kernel(dp_count, emb_ref, all_ref, send, recv):
    d = lax.axis_index("dp")
    f = lax.axis_index("fsdp")
    barrier = pltpu.get_barrier_semaphore()
    for k in range(1, dp_count):
        pl.semaphore_signal(
            barrier, inc=1, device_id=((d + k) % dp_count, f), device_id_type=pl.DeviceIdType.MESH
        )
    pl.semaphore_wait(barrier, dp_count - 1)

    def put(place, k, to):
        return pltpu.make_async_remote_copy(
            src_ref=emb_ref,
            dst_ref=all_ref.at[place],
            send_sem=send.at[k],
            recv_sem=recv.at[k],
            device_id=(to, f),
            device_id_type=pl.DeviceIdType.MESH,
        )

    copies = [put(d, k, (d + k) % dp_count) for k in range(1, dp_count)]
    for copy in copies:
        copy.start()
    all_ref[d] = emb_ref[...]
    for k in range(1, dp_count):
        put((d + dp_count - k) % dp_count, k, (d + k) % dp_count).wait_recv()
    for copy in copies:
        copy.wait_send()


def share(emb, dp_count):
    return pl.pallas_call(
        functools.partial(share_kernel, dp_count),
        out_shape=jax.ShapeDtypeStruct((dp_count,) + emb.shape, emb.dtype),
        in_specs=[pl.BlockSpec(memory_space=pltpu.VMEM)],
        out_specs=pl.BlockSpec(memory_space=pltpu.VMEM),
        scratch_shapes=[pltpu.SemaphoreType.DMA((dp_count,)), pltpu.SemaphoreType.DMA((dp_count,))],
        compiler_params=pltpu.CompilerParams(collective_id=1, has_side_effects=True),
    )(emb)


def body(
    page_embed,
    page_slot,
    doc_ids,
    qkv_weight,
    out_weight,
    fig_slot,
    cap_slot,
    logit_scale,
    loss_cotangent,
):
    dp_count = lax.axis_size("dp")
    me = lax.axis_index("dp")
    fs_count = lax.axis_size("fsdp")
    row_count, width = page_embed.shape
    capacity = -(-(5 * row_count) // (4 * dp_count))
    capacity = -(-capacity // 16) * 16
    total = dp_count * capacity
    pair_count = fig_slot.shape[0]
    hdim = qkv_weight.shape[2]
    owner_idx = page_slot // row_count
    slot_idx = page_slot % row_count
    onehot = (owner_idx[:, None] == jnp.arange(dp_count)[None, :]).astype(jnp.int32)
    rank_idx = jnp.sum((jnp.cumsum(onehot, axis=0) - onehot) * onehot, axis=1)
    place_idx = owner_idx * capacity + rank_idx
    place = jnp.arange(total)[:, None] == place_idx[None, :]
    send_ids = jnp.sum(jnp.where(place, slot_idx[None, :] + 1, 0), axis=1) - 1
    fixed_ct = (loss_cotangent * FIXED).astype(jnp.int32)
    send_ints = jnp.concatenate(
        [
            send_ids.reshape(dp_count, capacity),
            jnp.broadcast_to(fixed_ct[None, :], (dp_count, pair_count)),
        ],
        axis=1,
    )
    send_ints = jnp.pad(send_ints, ((0, 0), (0, -send_ints.shape[1] % 128)))
    send_ints = jnp.broadcast_to(send_ints[:, None], (dp_count, 8, send_ints.shape[1]))
    send_rows = mm(place.astype(BF), page_embed).astype(BF)
    rows, w_q, w_kv, w_out, recv_ints = move(
        send_rows, qkv_weight, out_weight, send_ints, dp_count, fs_count, capacity
    )
    recv_ints = recv_ints[:, 0]

    ids = recv_ints[:, :capacity].reshape(-1)
    group_ct = recv_ints[:, capacity : capacity + pair_count].reshape(-1).astype(F32) * (1.0 / FIXED)
    doc_row = doc_ids[0]
    slot_range = jnp.arange(row_count)
    row_docs = (
        jnp.sum(jnp.where(ids[:, None] == slot_range[None, :], doc_row[None, :] + 1, 0), axis=1) - 1
    )
    slots = jnp.concatenate([fig_slot, cap_slot])
    slot_docs = jnp.sum(jnp.where(slots[:, None] == slot_range[None, :], doc_row[None, :], 0), axis=1)
    picked = (slots[:, None] == ids[None, :]).astype(BF)
    same_doc = slot_docs[:, None] == row_docs[None, :]
    pick_count = slots.shape[0]

    picked_rows = mm(picked, rows).astype(BF)
    scale = 1.0 / math.sqrt(HD)
    heads = hdim // HD
    head_mask = (
        jnp.arange(hdim)[None, None, :] // HD == jnp.arange(heads)[:, None, None]
    ).astype(F32)

    key_value = mm(rows, w_kv).astype(BF)
    key, value = key_value[:, :hdim], key_value[:, hdim:]
    query = expand(mm(picked_rows, w_q).astype(BF), head_mask)
    scores = mmt(query, key).reshape(heads, pick_count, total) * scale
    weights = jnp.exp(jnp.where(same_doc[None], scores, -1e30))
    prob = weights / jnp.sum(weights, axis=2, keepdims=True)
    prob_b = prob.astype(BF).reshape(heads * pick_count, total)
    mixed = collapse(mm(prob_b, value), head_mask, pick_count).astype(BF)
    attn_out = mm(mixed, w_out)

    vec = picked_rows.astype(F32) + attn_out
    inv = lax.rsqrt(jnp.sum(vec * vec, axis=1, keepdims=True) + EPSILON)
    unit = vec * inv
    all_emb = share(unit.astype(BF), dp_count)
    all_fig = all_emb[:, :pair_count].reshape(-1, width)
    all_cap = all_emb[:, pair_count:].reshape(-1, width)
    logit_mult = logit_scale[0]
    logits = logit_mult * mmt(all_fig, all_cap)
    row_lse = jnp.log(jnp.sum(jnp.exp(logits), axis=1))
    col_lse = jnp.log(jnp.sum(jnp.exp(logits), axis=0))
    group_pairs = logits.shape[0]
    eye = jnp.arange(group_pairs)[:, None] == jnp.arange(group_pairs)[None, :]
    diag = jnp.sum(jnp.where(eye, logits, 0.0), axis=1)
    eye = eye.astype(F32)
    all_loss = 0.5 * (row_lse - diag) + 0.5 * (col_lse - diag)
    pair_loss = lax.dynamic_slice_in_dim(all_loss, me * pair_count, pair_count, 0)
    coef = 0.5 * group_ct[:, None] * (jnp.exp(logits - row_lse[:, None]) - eye) + 0.5 * (
        jnp.exp(logits - col_lse[None, :]) - eye
    ) * group_ct[None, :]
    coef_f = lax.dynamic_slice_in_dim(coef, me * pair_count, pair_count, 0)
    coef_c = lax.dynamic_slice_in_dim(coef.T, me * pair_count, pair_count, 0)
    grad = logit_mult * jnp.concatenate(
        [exact_mm(coef_f, all_cap), exact_mm(coef_c, all_fig)], axis=0
    )
    dvec = inv * (grad - unit * jnp.sum(unit * grad, axis=1, keepdims=True))

    dmix = expand(mmt(dvec.astype(BF), w_out).astype(BF), head_mask)
    dprob = mmt(dmix, value).reshape(heads, pick_count, total)
    dscore = prob * (dprob - jnp.sum(dprob * prob, axis=2, keepdims=True)) * scale
    dscore = dscore.astype(BF).reshape(heads * pick_count, total)
    dquery = collapse(mm(dscore, key), head_mask, pick_count).astype(BF)
    picked_ct = dvec + mmt(dquery, w_q)
    dkey_value = jnp.concatenate(
        [tmm(dscore, query).astype(BF), tmm(prob_b, dmix).astype(BF)], axis=1
    )
    ct_hi = picked_ct.astype(BF)
    ct_lo = (picked_ct - ct_hi.astype(F32)).astype(BF)
    row_ct = mmt(dkey_value, w_kv) + tmm(
        jnp.concatenate([picked, picked], axis=0), jnp.concatenate([ct_hi, ct_lo], axis=0)
    )
    home = lax.all_to_all(row_ct.astype(BF), "dp", split_axis=0, concat_axis=0, tiled=True)
    page_grad = tmm(place.astype(BF), home).astype(BF)
    return (page_grad, pair_loss)


def solution(mesh):
    return jax.shard_map(
        body,
        mesh=mesh,
        in_specs=(
            P(("dp", "fsdp"), None),
            P(("dp", "fsdp")),
            P(("dp", "fsdp"), None),
            P(None, "fsdp", None),
            P(None, "fsdp"),
            P(("dp", "fsdp")),
            P(("dp", "fsdp")),
            P(),
            P(("dp", "fsdp")),
        ),
        out_specs=(P(("dp", "fsdp"), None), P(("dp", "fsdp"))),
        check_vma=False,
    )
```
